32 devices in a mesh: vocab: 16 (over z, y, core), width: 2 (over x).
Axes of the slice: x: 2, y: 2, z: 4, core: 2. Of those that a mesh axis runs over, the one named last changes fastest.
Arguments:
- hidden: bfloat16 [128, 4608], P('vocab', 'width'), may hold values from -72 to 72
- pre_gain: float32 [4608], P('width'), may hold values from 0.1 to 1.9
- post_gain: float32 [4608], P('width'), may hold values from 0.1 to 1.9
- final_gain: float32 [4608], P('width'), may hold values from 0.1 to 1.9
- gate_weight: bfloat16 [4608, 18432], P('width', 'vocab'), may hold values from -0.09375 to 0.09375
- up_weight: bfloat16 [4608, 18432], P('width', 'vocab'), may hold values from -0.09375 to 0.09375
- down_weight: bfloat16 [18432, 4608], P('vocab', 'width'), may hold values from -2 to 2
- head_weight: bfloat16 [4608, 65536], P('width', 'vocab'), may hold values from -0.25 to 0.25
- token_ids: int32 [128], replicated, may hold values from 0 to 65535
- rewards: float32 [16], replicated, may hold values from -3 to 3
Outputs:
- grad_hidden: bfloat16 [128, 4608], P('vocab', 'width')
- grad_gate: bfloat16 [4608, 18432], P('width', 'vocab')
- grad_up: bfloat16 [4608, 18432], P('width', 'vocab')
- grad_down: bfloat16 [18432, 4608], P('vocab', 'width')
- grad_head: bfloat16 [4608, 65536], P('width', 'vocab')
- loss: float32 [], replicated
The draws below stay inside these ranges and needn't reach their ends.
All inputs are finite; a program needn't handle non-finite values.
Results may differ from the reference program's by a relative error of at most 0.013.
Values may be sent and summed in bfloat16 or wider, within the bound.
A program may use at most 128 MiB of HBM per device.

```python
import math
import jax
import jax.numpy as jnp
from jax import lax

D = 4608
FF = 18432
VOCAB_DEV = 4096
LEN = 8
CAP = 30
TOKENS = 128
SEQS = 16
VOCAB = 65536


def draw_hidden(key, part):
    key_rows = jax.random.fold_in(key, 11)
    key_cols = jax.random.fold_in(key, 12)
    key_base = jax.random.fold_in(key, 13)
    row_scale = 0.3 * jnp.exp(jax.random.uniform(key_rows, (TOKENS, 1), jnp.float32, 0.0, math.log(10.0)))
    position = jnp.arange(D, dtype=jnp.float32)[None, :] / (D - 1)
    rough = jnp.exp(jax.random.uniform(key_cols, (1, D), jnp.float32, 0.0, math.log(4.0)))
    rising = jnp.exp(math.log(2.5) * position)
    base = jnp.clip(jax.random.normal(key_base, (TOKENS, D), jnp.float32), -6.0, 6.0)
    col_scale = 0.4 * rising * rough
    return (base * row_scale * col_scale).astype(jnp.bfloat16)


def draw_down_weight(key, part):
    key_base = jax.random.fold_in(key, 21)
    position = jnp.arange(D, dtype=jnp.float32)[None, :] / (D - 1) - 0.5
    rising = jnp.exp(math.log(2.5) * position)
    base = jnp.clip(jax.random.normal(key_base, (FF, D), jnp.float32), -6.0, 6.0)
    return (base * rising / math.sqrt(FF)).astype(jnp.bfloat16)


def with_ends(result, rng, smallest, high):
    longest = result.shape.index(max(result.shape))
    spots = []
    for shift in (0, 1):
        where = [jax.random.randint(jax.random.fold_in(rng, axis), (), 0, length) for axis, length in enumerate(result.shape)]
        where[longest] = (where[longest] + shift) % result.shape[longest]
        spots.append(tuple(where))
    return result.at[spots[0]].set(smallest).at[spots[1]].set(high)


def shard_levels(stream_key, shape, pieces, least, top_value):
    def one(axis_at, parts):
        steps = jax.random.uniform(jax.random.fold_in(jax.random.fold_in(stream_key, 6), axis_at), (parts,), jnp.float32, least / len(pieces), top_value / len(pieces))
        return jnp.repeat(jnp.exp(steps), shape[axis_at] // parts).reshape((-1,) + (1,) * (len(shape) - axis_at - 1))

    gain = one(*pieces[0])
    for cut in pieces[1:]:
        gain = gain * one(*cut)
    return gain


def normal_values(own_key, extent, width, limit, shards=(), kind=jnp.bfloat16):
    entries = width * jax.random.normal(own_key, extent, jnp.float32)
    if shards:
        entries = entries * shard_levels(own_key, extent, shards, -0.22, 0.18)
    return jnp.clip(entries, -limit, limit).astype(kind)


def setup_inputs(seed: int = 0) -> dict:
    key_list = jax.random.split(jax.random.key(seed), 11)
    hidden = draw_hidden(jax.random.fold_in(key_list[10], 71), 0)
    pre_gain = jnp.clip(1.0 + 0.18 * jax.random.normal(key_list[1], (D,), jnp.float32), 0.1, 1.9)
    post_gain = jnp.clip(1.0 + 0.18 * jax.random.normal(key_list[2], (D,), jnp.float32), 0.1, 1.9)
    final_gain = jnp.clip(1.0 + 0.18 * jax.random.normal(key_list[3], (D,), jnp.float32), 0.1, 1.9)
    gate_weight = normal_values(key_list[4], (D, FF), D ** -0.5, 0.09375, ((0, 2), (1, 16)))
    up_weight = normal_values(key_list[5], (D, FF), D ** -0.5, 0.09375, ((0, 2), (1, 16)))
    down_weight = draw_down_weight(jax.random.fold_in(key_list[10], 71), 0)
    head_weight = normal_values(key_list[7], (D, VOCAB), (D // 9) ** -0.5, 0.25, ((0, 2), (1, 16)))
    token_ids = with_ends(jax.random.randint(key_list[8], (TOKENS,), 0, VOCAB), jax.random.fold_in(key_list[8], 1), 0, VOCAB - 1).astype(jnp.int32)
    rewards = normal_values(key_list[9], (SEQS,), 1.0, 3.0, (), jnp.float32)
    return {"hidden": hidden, "pre_gain": pre_gain, "post_gain": post_gain, "final_gain": final_gain, "gate_weight": gate_weight, "up_weight": up_weight, "down_weight": down_weight, "head_weight": head_weight, "token_ids": token_ids, "rewards": rewards}


EPS = 1e-06
ROOT_TWO_PI = math.sqrt(2.0 / math.pi)

def gelu_value(value):
    inner = ROOT_TWO_PI * (value + 0.044715 * value * value * value)
    return 0.5 * value * (1.0 + jnp.tanh(inner))

def gelu_slope(value):
    bent = jnp.tanh(ROOT_TWO_PI * (value + 0.044715 * value * value * value))
    return 0.5 * (1.0 + bent) + 0.5 * value * (1.0 - bent * bent) * ROOT_TWO_PI * (1.0 + 3.0 * 0.044715 * value * value)

def reference(hidden, pre_gain, post_gain, final_gain, gate_weight, up_weight, down_weight, head_weight, token_ids, rewards):
    inputs = hidden.astype(jnp.float32)
    model = inputs.shape[1]
    scale_pre = lax.rsqrt(lax.optimization_barrier(jnp.sum(inputs * inputs, axis=1, keepdims=True)) / model + EPS)
    normed = (inputs * scale_pre * pre_gain).astype(jnp.bfloat16)
    gate = jnp.dot(normed, gate_weight, preferred_element_type=jnp.float32)
    upward = jnp.dot(normed, up_weight, preferred_element_type=jnp.float32)
    gelu_gate = gelu_value(gate)
    active = (gelu_gate * upward).astype(jnp.bfloat16)
    branch = jnp.dot(active, down_weight, preferred_element_type=jnp.float32)
    scale_post = lax.rsqrt(lax.optimization_barrier(jnp.sum(branch * branch, axis=1, keepdims=True)) / model + EPS)
    resid = inputs + branch * scale_post * post_gain
    scale_final = lax.rsqrt(lax.optimization_barrier(jnp.sum(resid * resid, axis=1, keepdims=True)) / model + EPS)
    final = (resid * scale_final * final_gain).astype(jnp.bfloat16)
    blocks_count = VOCAB // VOCAB_DEV
    blocks = jnp.moveaxis(head_weight.reshape(model, blocks_count, VOCAB_DEV), 1, 0)
    columns = jnp.arange(VOCAB, dtype=jnp.int32).reshape(blocks_count, VOCAB_DEV)

    def capped_block(block):
        logits = jnp.dot(final, block, preferred_element_type=jnp.float32)
        return CAP * jnp.tanh(logits / CAP)
    capped = lax.map(capped_block, blocks)
    hits = columns[:, None, :] == token_ids[None, :, None]
    total = lax.optimization_barrier(jnp.sum(jnp.exp(capped - CAP), axis=(0, 2)))
    target = lax.optimization_barrier(jnp.sum(jnp.where(hits, capped, 0.0), axis=(0, 2)))
    lognorm = CAP + jnp.log(total)
    logprob = target - lognorm
    weights = jnp.repeat(rewards, LEN)
    loss = -jnp.mean(weights * logprob)

    def second_pass(carry, item):
        block, capped_part, hit_part = item
        prob = jnp.exp(capped_part - lognorm[:, None])
        slope = 1.0 - (capped_part / CAP) ** 2
        delta = (-weights[:, None] * (hit_part.astype(jnp.float32) - prob) * slope).astype(jnp.bfloat16)
        grad_block = lax.dot_general(final, delta, (((0,), (0,)), ((), ())), preferred_element_type=jnp.float32).astype(jnp.bfloat16)
        carry = carry + lax.dot_general(delta, block, (((1,), (1,)), ((), ())), preferred_element_type=jnp.float32)
        return (carry, grad_block)
    grad_final, grad_blocks = lax.scan(second_pass, jnp.zeros(final.shape, jnp.float32), (blocks, capped, hits))
    grad_head = jnp.moveaxis(grad_blocks, 0, 1).reshape(model, VOCAB)
    weighted = grad_final * final_gain
    back_final = lax.optimization_barrier(jnp.sum(weighted * resid, axis=1, keepdims=True))
    grad_resid = scale_final * weighted - resid * scale_final ** 3 * back_final / model
    weighted_post = grad_resid * post_gain
    back_post = lax.optimization_barrier(jnp.sum(weighted_post * branch, axis=1, keepdims=True))
    grad_branch = (scale_post * weighted_post - branch * scale_post ** 3 * back_post / model).astype(jnp.bfloat16)
    grad_down = lax.dot_general(active, grad_branch, (((0,), (0,)), ((), ())), preferred_element_type=jnp.float32).astype(jnp.bfloat16)
    grad_active = lax.dot_general(grad_branch, down_weight, (((1,), (1,)), ((), ())), preferred_element_type=jnp.float32)
    grad_gate_in = (grad_active * upward * gelu_slope(gate)).astype(jnp.bfloat16)
    grad_up_in = (grad_active * gelu_gate).astype(jnp.bfloat16)
    grad_gate = lax.dot_general(normed, grad_gate_in, (((0,), (0,)), ((), ())), preferred_element_type=jnp.float32).astype(jnp.bfloat16)
    grad_up = lax.dot_general(normed, grad_up_in, (((0,), (0,)), ((), ())), preferred_element_type=jnp.float32).astype(jnp.bfloat16)
    grad_normed = lax.dot_general(grad_gate_in, gate_weight, (((1,), (1,)), ((), ())), preferred_element_type=jnp.float32)
    grad_normed = grad_normed + lax.dot_general(grad_up_in, up_weight, (((1,), (1,)), ((), ())), preferred_element_type=jnp.float32)
    weighted_pre = grad_normed * pre_gain
    back_pre = lax.optimization_barrier(jnp.sum(weighted_pre * inputs, axis=1, keepdims=True))
    grad_hidden = (grad_resid + scale_pre * weighted_pre - inputs * scale_pre ** 3 * back_pre / model).astype(jnp.bfloat16)
    return (grad_hidden, grad_gate, grad_up, grad_down, grad_head, loss)
```

```python
import functools
import math

import jax
import jax.numpy as jnp
from jax import lax
from jax.experimental import pallas as pl
from jax.experimental.pallas import tpu as pltpu
from jax.sharding import PartitionSpec as P

CAP = 30
EPS = 1e-06
ROOT_TWO_PI = math.sqrt(2.0 / math.pi)
MESH = pl.DeviceIdType.MESH
F32 = jnp.float32
BF16 = jnp.bfloat16
DMA = pltpu.SemaphoreType.DMA
LIMIT = 48 * 1024 * 1024


def contract(left, right, left_dim, right_dim):
    return lax.dot_general(
        left, right, (((left_dim,), (right_dim,)), ((), ())), preferred_element_type=F32
    )


def place():
    return lax.axis_index("vocab"), lax.axis_index("width")


def greet(devices):
    barrier = pltpu.get_barrier_semaphore()
    for device in devices:
        pl.semaphore_signal(barrier, inc=1, device_id=device, device_id_type=MESH)
    pl.semaphore_wait(barrier, len(devices))


def remote(src, dst, send_sem, recv_sem, device):
    return pltpu.make_async_remote_copy(
        src_ref=src,
        dst_ref=dst,
        send_sem=send_sem,
        recv_sem=recv_sem,
        device_id=device,
        device_id_type=MESH,
    )


def row_peers(nw):
    v, w = place()
    return [(v, lax.rem(w + k, nw)) for k in range(1, nw)]


def column_peers(nv):
    v, w = place()
    chips = nv // 2
    chip, core = v // 2, lax.rem(v, 2)
    same = [(lax.rem(chip + k, chips) * 2 + core, w) for k in range(1, chips)]
    return [(chip * 2 + 1 - core, w)] + same


def row_sum(value, slots, send, recv, nw):
    v, w = place()
    slots[w] = jnp.broadcast_to(value, slots.shape[1:])
    copies = []
    for k in range(1, nw):
        copy = remote(slots.at[w], slots.at[w], send.at[k], recv.at[k], (v, lax.rem(w + k, nw)))
        copy.start()
        copies.append(copy)
    for copy in copies:
        copy.wait()
    return jnp.sum(slots[...], axis=0)[:, :1]


def gather_rows(out, send, recv, near_send, near_recv, nv):
    v, w = place()
    chips = nv // 2
    chip, core = v // 2, lax.rem(v, 2)
    sibling = (chip * 2 + 1 - core, w)
    far, near = [], []
    for k in range(1, chips):
        target = (lax.rem(chip + k, chips) * 2 + core, w)
        copy = remote(out.at[v], out.at[v], send.at[k], recv.at[k], target)
        copy.start()
        far.append(copy)
    copy = remote(out.at[v], out.at[v], near_send.at[0], near_recv.at[0], sibling)
    copy.start()
    near.append(copy)
    for k in range(1, chips):
        source = lax.rem(chip + chips - k, chips) * 2 + core
        far[k - 1].wait_recv()
        copy = remote(out.at[source], out.at[source], near_send.at[k], near_recv.at[k], sibling)
        copy.start()
        near.append(copy)
    for copy in near:
        copy.wait_recv()
    for copy in far + near:
        copy.wait_send()


def scatter_sum(part, paired, stage, land, send, recv, near_send, near_recv, nv):
    v, w = place()
    chips = nv // 2
    chip, core = v // 2, lax.rem(v, 2)
    sibling = (chip * 2 + 1 - core, w)
    near, far = [None] * chips, []
    order = list(range(1, chips)) + [0]
    for k in order:
        to_chip = lax.rem(chip + k, chips)
        copy = remote(
            part.at[to_chip, 1 - core], paired.at[k], near_send.at[k], near_recv.at[k], sibling
        )
        copy.start()
        near[k] = copy
    total = None
    for k in order:
        to_chip = lax.rem(chip + k, chips)
        near[k].wait_recv()
        both = part[to_chip, core].astype(F32) + paired[k].astype(F32)
        if k == 0:
            total = both
        else:
            stage[k] = both.astype(BF16)
            copy = remote(stage.at[k], land.at[k], send.at[k], recv.at[k], (to_chip * 2 + core, w))
            copy.start()
            far.append(copy)
    for k in range(1, chips):
        far[k - 1].wait_recv()
        total = total + land[k].astype(F32)
    for copy in near + far:
        copy.wait_send()
    return total


def pre_kernel(nv, nw, model, hidden, gain, normed, scale, slots, ss, sr, gs, gr, hs, hr):
    v, _ = place()
    greet(column_peers(nv) + row_peers(nw))
    inputs = hidden[...].astype(F32)
    squares = row_sum(jnp.sum(inputs * inputs, axis=1, keepdims=True), slots, ss, sr, nw)
    factor = lax.rsqrt(squares / model + EPS)
    scale[...] = jnp.broadcast_to(factor, scale.shape)
    normed[v] = (inputs * factor * gain[...]).astype(BF16)
    gather_rows(normed, gs, gr, hs, hr, nv)


def gate_kernel(nw, gate_part, up_part, active, value, slope, mine, land, send, recv):
    v, w = place()
    greet(row_peers(nw))
    copies = []
    for half, part in enumerate((gate_part, up_part)):
        mine[half] = part[...].astype(BF16)
        for k in range(1, nw):
            copy = remote(
                mine.at[half],
                land.at[k - 1, half],
                send.at[k, half],
                recv.at[k, half],
                (v, lax.rem(w + k, nw)),
            )
            copy.start()
            copies.append(copy)
    gate, upward = gate_part[...], up_part[...]
    for copy in copies:
        copy.wait()
    for k in range(nw - 1):
        gate = gate + land[k, 0].astype(F32)
        upward = upward + land[k, 1].astype(F32)
    bent = jnp.tanh(ROOT_TWO_PI * (gate + 0.044715 * gate * gate * gate))
    gelu = 0.5 * gate * (1.0 + bent)
    active[...] = (gelu * upward).astype(BF16)
    value[...] = gelu
    slope[...] = upward * (
        0.5 * (1.0 + bent)
        + 0.5 * gate * (1.0 - bent * bent) * ROOT_TWO_PI * (1.0 + 3.0 * 0.044715 * gate * gate)
    )


def post_kernel(
    nv, nw, model,
    part, hidden, post_gain, final_gain,
    final, branch_out, resid_out, scales,
    paired, stage, land, slots, slots_two,
    ss, sr, ts, tr, gs, gr, hs, hr, ps, pr, qs, qr,
):
    v, _ = place()
    greet(column_peers(nv) + row_peers(nw))
    branch = scatter_sum(part, paired, stage, land, ps, pr, qs, qr, nv)
    squares = row_sum(jnp.sum(branch * branch, axis=1, keepdims=True), slots, ss, sr, nw)
    scale_post = lax.rsqrt(squares / model + EPS)
    resid = hidden[...].astype(F32) + branch * scale_post * post_gain[...]
    squares = row_sum(jnp.sum(resid * resid, axis=1, keepdims=True), slots_two, ts, tr, nw)
    scale_final = lax.rsqrt(squares / model + EPS)
    final[v] = (resid * scale_final * final_gain[...]).astype(BF16)
    branch_out[...] = branch
    resid_out[...] = resid
    scales[0] = jnp.broadcast_to(scale_post, scales.shape[1:])
    scales[1] = jnp.broadcast_to(scale_final, scales.shape[1:])
    gather_rows(final, gs, gr, hs, hr, nv)


def head_kernel(
    nv, nw,
    logits, ids, weights,
    delta, loss,
    mine, land, col_slots, row_slots, capped,
    xs, xr, cs, cr, rs, rr, ds, dr,
):
    v, w = place()
    sub, tokens = logits.shape[1:]
    column = [(lax.rem(v + k, nv), w) for k in range(1, nv)]
    row = row_peers(nw)
    greet(column + row)
    copies = []
    for k in range(1, nw):
        peer = lax.rem(w + k, nw)
        mine[k - 1] = logits[peer].astype(BF16)
        copy = remote(mine.at[k - 1], land.at[k - 1], xs.at[k], xr.at[k], (v, peer))
        copy.start()
        copies.append(copy)
    for copy in copies:
        copy.wait()
    total = logits[w]
    for k in range(nw - 1):
        total = total + land[k].astype(F32)
    cap = CAP * jnp.tanh(total / CAP)
    capped[...] = cap
    first = (v * nw + w) * sub
    hits = (lax.broadcasted_iota(jnp.int32, (sub, tokens), 0) + first) == ids[...]
    sums = jnp.sum(jnp.exp(cap - CAP), axis=0, keepdims=True)
    marks = jnp.sum(jnp.where(hits, cap, 0.0), axis=0, keepdims=True)
    which = lax.broadcasted_iota(jnp.int32, (8, tokens), 0)
    col_slots[v] = jnp.where(which == 0, sums, jnp.where(which == 1, marks, 0.0))
    copies = []
    for k in range(1, nv):
        copy = remote(col_slots.at[v], col_slots.at[v], cs.at[k], cr.at[k], column[k - 1])
        copy.start()
        copies.append(copy)
    for copy in copies:
        copy.wait()
    row_slots[w] = jnp.sum(col_slots[...], axis=0)
    copies = []
    for k in range(1, nw):
        copy = remote(row_slots.at[w], row_slots.at[w], rs.at[k], rr.at[k], row[k - 1])
        copy.start()
        copies.append(copy)
    for copy in copies:
        copy.wait()
    both = jnp.sum(row_slots[...], axis=0)
    lognorm = CAP + jnp.log(both[0:1])
    weight = weights[...]
    logprob = both[1:2] - lognorm
    mean = -jnp.sum(weight * logprob, axis=1, keepdims=True) / tokens
    loss[...] = jnp.broadcast_to(mean, loss.shape)
    cap = capped[...]
    prob = jnp.exp(cap - lognorm)
    slope = 1.0 - (cap / CAP) ** 2
    delta[w] = (-weight * (jnp.where(hits, 1.0, 0.0) - prob) * slope).astype(BF16)
    copies = []
    for k in range(1, nw):
        copy = remote(delta.at[w], delta.at[w], ds.at[k], dr.at[k], row[k - 1])
        copy.start()
        copies.append(copy)
    for copy in copies:
        copy.wait()


def turn_kernel(
    nv, nw, model,
    part, branch_ref, resid_ref, scales, post_gain, final_gain,
    grad_branch, grad_resid_out,
    paired, stage, land, slots, slots_two,
    ss, sr, ts, tr, gs, gr, hs, hr, ps, pr, qs, qr,
):
    v, _ = place()
    greet(column_peers(nv) + row_peers(nw))
    grad_final = scatter_sum(part, paired, stage, land, ps, pr, qs, qr, nv)
    resid, branch = resid_ref[...], branch_ref[...]
    scale_post, scale_final = scales[0][:, :1], scales[1][:, :1]
    weighted = grad_final * final_gain[...]
    back = row_sum(jnp.sum(weighted * resid, axis=1, keepdims=True), slots, ss, sr, nw)
    grad_resid = scale_final * weighted - resid * (
        scale_final * scale_final * scale_final * back / model
    )
    weighted = grad_resid * post_gain[...]
    back = row_sum(jnp.sum(weighted * branch, axis=1, keepdims=True), slots_two, ts, tr, nw)
    grad_branch[v] = (
        scale_post * weighted - branch * (scale_post * scale_post * scale_post * back / model)
    ).astype(BF16)
    grad_resid_out[...] = grad_resid
    gather_rows(grad_branch, gs, gr, hs, hr, nv)


def active_kernel(nw, part, value, slope, gate_in, up_in, mine, land, send, recv):
    v, w = place()
    greet(row_peers(nw))
    mine[...] = part[...].astype(BF16)
    copies = []
    for k in range(1, nw):
        copy = remote(mine, land.at[k - 1], send.at[k], recv.at[k], (v, lax.rem(w + k, nw)))
        copy.start()
        copies.append(copy)
    for copy in copies:
        copy.wait()
    total = part[...]
    for k in range(nw - 1):
        total = total + land[k].astype(F32)
    gate_in[...] = (total * slope[...]).astype(BF16)
    up_in[...] = (total * value[...]).astype(BF16)


def tail_kernel(
    nv, nw, model,
    part, hidden, pre_gain, scale, grad_resid,
    out,
    paired, stage, land, slots,
    ss, sr, ps, pr, qs, qr,
):
    greet(column_peers(nv) + row_peers(nw))
    grad_normed = scatter_sum(part, paired, stage, land, ps, pr, qs, qr, nv)
    inputs = hidden[...].astype(F32)
    factor = scale[...][:, :1]
    weighted = grad_normed * pre_gain[...]
    back = row_sum(jnp.sum(weighted * inputs, axis=1, keepdims=True), slots, ss, sr, nw)
    out[...] = (
        grad_resid[...]
        + factor * weighted
        - inputs * (factor * factor * factor * back / model)
    ).astype(BF16)


def call(kernel, number, outs, scratch, name):
    vmem = pl.BlockSpec(memory_space=pltpu.VMEM)

    def run(*operands):
        return pl.pallas_call(
            kernel,
            out_shape=tuple(jax.ShapeDtypeStruct(shape, kind) for shape, kind in outs),
            in_specs=[vmem] * len(operands),
            out_specs=tuple(vmem for _ in outs),
            scratch_shapes=scratch,
            compiler_params=pltpu.CompilerParams(
                collective_id=number, has_side_effects=True, vmem_limit_bytes=LIMIT
            ),
            name=name,
        )(*operands)

    return run


def shards(
    hidden,
    pre_gain,
    post_gain,
    final_gain,
    gate_weight,
    up_weight,
    down_weight,
    head_weight,
    token_ids,
    rewards,
):
    nv, nw = lax.axis_size("vocab"), lax.axis_size("width")
    own, wide = hidden.shape
    model = wide * nw
    tokens = nv * own
    chips = nv // 2
    units = gate_weight.shape[1]
    vocab_dev = head_weight.shape[1]
    sub = vocab_dev // nw
    pre_gain, post_gain, final_gain = (g[None, :] for g in (pre_gain, post_gain, final_gain))

    sums = pltpu.VMEM((nw, own, 128), F32)
    row_sems = [DMA((nw,)), DMA((nw,))]
    chip_sems = [DMA((chips,)), DMA((chips,))]
    block = pltpu.VMEM((chips, own, wide), BF16)
    gather_sems = chip_sems * 2

    normed, scale = call(
        functools.partial(pre_kernel, nv, nw, model),
        0,
        [((nv, own, wide), BF16), ((own, 128), F32)],
        [sums] + row_sems + gather_sems,
        "pre_norm",
    )(hidden, pre_gain)
    normed = normed.reshape(tokens, wide)
    gate_part = jnp.dot(normed, gate_weight, preferred_element_type=F32)
    up_part = jnp.dot(normed, up_weight, preferred_element_type=F32)
    active, value, slope = call(
        functools.partial(gate_kernel, nw),
        1,
        [((tokens, units), BF16), ((tokens, units), F32), ((tokens, units), F32)],
        [
            pltpu.VMEM((2, tokens, units), BF16),
            pltpu.VMEM((nw - 1, 2, tokens, units), BF16),
            DMA((nw, 2)),
            DMA((nw, 2)),
        ],
        "gate_sum",
    )(gate_part, up_part)
    branch_part = jnp.dot(active, down_weight, preferred_element_type=F32).astype(BF16)
    final, branch, resid, scales = call(
        functools.partial(post_kernel, nv, nw, model),
        2,
        [((nv, own, wide), BF16), ((own, wide), F32), ((own, wide), F32), ((2, own, 128), F32)],
        [block, block, block, sums, sums] + row_sems * 2 + gather_sems + chip_sems * 2,
        "post_norm",
    )(branch_part.reshape(chips, 2, own, wide), hidden, post_gain, final_gain)
    final = final.reshape(tokens, wide)
    logits = contract(head_weight, final, 0, 1).reshape(nw, sub, tokens)
    weights = jnp.repeat(rewards, tokens // rewards.shape[0])[None, :]
    delta, loss = call(
        functools.partial(head_kernel, nv, nw),
        3,
        [((nw, sub, tokens), BF16), ((8, 128), F32)],
        [
            pltpu.VMEM((nw - 1, sub, tokens), BF16),
            pltpu.VMEM((nw - 1, sub, tokens), BF16),
            pltpu.VMEM((nv, 8, tokens), F32),
            pltpu.VMEM((nw, 8, tokens), F32),
            pltpu.VMEM((sub, tokens), F32),
        ]
        + row_sems
        + [DMA((nv,)), DMA((nv,))]
        + row_sems * 2,
        "head_loss",
    )(logits, token_ids[None, :], weights)
    delta = delta.reshape(vocab_dev, tokens)
    final_part = contract(delta, head_weight, 0, 1).astype(BF16)
    grad_branch, grad_resid = call(
        functools.partial(turn_kernel, nv, nw, model),
        4,
        [((nv, own, wide), BF16), ((own, wide), F32)],
        [block, block, block, sums, sums] + row_sems * 2 + gather_sems + chip_sems * 2,
        "turn",
    )(final_part.reshape(chips, 2, own, wide), branch, resid, scales, post_gain, final_gain)
    grad_branch = grad_branch.reshape(tokens, wide)
    active_part = contract(grad_branch, down_weight, 1, 1)
    gate_in, up_in = call(
        functools.partial(active_kernel, nw),
        5,
        [((tokens, units), BF16), ((tokens, units), BF16)],
        [
            pltpu.VMEM((tokens, units), BF16),
            pltpu.VMEM((nw - 1, tokens, units), BF16),
        ]
        + row_sems,
        "active_sum",
    )(active_part, value, slope)
    normed_part = (
        contract(gate_in, gate_weight, 1, 1) + contract(up_in, up_weight, 1, 1)
    ).astype(BF16)
    (grad_hidden,) = call(
        functools.partial(tail_kernel, nv, nw, model),
        6,
        [((own, wide), BF16)],
        [block, block, block, sums] + row_sems + chip_sems * 2,
        "tail",
    )(normed_part.reshape(chips, 2, own, wide), hidden, pre_gain, scale, grad_resid)
    grad_head = contract(final, delta, 0, 1).astype(BF16)
    grad_down = contract(active, grad_branch, 0, 0).astype(BF16)
    grad_gate = contract(normed, gate_in, 0, 0).astype(BF16)
    grad_up = contract(normed, up_in, 0, 0).astype(BF16)
    return (grad_hidden, grad_gate, grad_up, grad_down, grad_head, loss[0, 0])


def solution(mesh):
    return jax.shard_map(
        shards,
        mesh=mesh,
        in_specs=(
            P("vocab", "width"),
            P("width"),
            P("width"),
            P("width"),
            P("width", "vocab"),
            P("width", "vocab"),
            P("vocab", "width"),
            P("width", "vocab"),
            P(),
            P(),
        ),
        out_specs=(
            P("vocab", "width"),
            P("width", "vocab"),
            P("width", "vocab"),
            P("vocab", "width"),
            P("width", "vocab"),
            P(),
        ),
        check_vma=False,
    )
```

```python
import functools
import math

import jax
import jax.numpy as jnp
from jax import lax
from jax.experimental import pallas as pl
from jax.experimental.pallas import tpu as pltpu
from jax.sharding import PartitionSpec as P

CAP = 30
EPS = 1e-06
ROOT_TWO_PI = math.sqrt(2.0 / math.pi)
MESH = pl.DeviceIdType.MESH
F32 = jnp.float32
BF16 = jnp.bfloat16
DMA = pltpu.SemaphoreType.DMA
LIMIT = 48 * 1024 * 1024


def contract(left, right, left_dim, right_dim):
    return lax.dot_general(
        left, right, (((left_dim,), (right_dim,)), ((), ())), preferred_element_type=F32
    )


def place():
    return lax.axis_index("vocab"), lax.axis_index("width")


def greet(devices):
    barrier = pltpu.get_barrier_semaphore()
    for device in devices:
        pl.semaphore_signal(barrier, inc=1, device_id=device, device_id_type=MESH)
    pl.semaphore_wait(barrier, len(devices))


def remote(src, dst, send_sem, recv_sem, device):
    return pltpu.make_async_remote_copy(
        src_ref=src,
        dst_ref=dst,
        send_sem=send_sem,
        recv_sem=recv_sem,
        device_id=device,
        device_id_type=MESH,
    )


def row_peers(nw):
    v, w = place()
    return [(v, lax.rem(w + k, nw)) for k in range(1, nw)]


def column_peers(nv):
    v, w = place()
    chips = nv // 2
    chip, core = v // 2, lax.rem(v, 2)
    same = [(lax.rem(chip + k, chips) * 2 + core, w) for k in range(1, chips)]
    return [(chip * 2 + 1 - core, w)] + same


def row_sum(value, slots, send, recv, nw):
    v, w = place()
    slots[w] = jnp.broadcast_to(value, slots.shape[1:])
    copies = []
    for k in range(1, nw):
        copy = remote(slots.at[w], slots.at[w], send.at[k], recv.at[k], (v, lax.rem(w + k, nw)))
        copy.start()
        copies.append(copy)
    for copy in copies:
        copy.wait()
    return jnp.sum(slots[...], axis=0)[:, :1]


def gather_rows(out, send, recv, near_send, near_recv, nv):
    v, w = place()
    chips = nv // 2
    chip, core = v // 2, lax.rem(v, 2)
    sibling = (chip * 2 + 1 - core, w)
    far, near = [], []
    for k in range(1, chips):
        target = (lax.rem(chip + k, chips) * 2 + core, w)
        copy = remote(out.at[v], out.at[v], send.at[k], recv.at[k], target)
        copy.start()
        far.append(copy)
    copy = remote(out.at[v], out.at[v], near_send.at[0], near_recv.at[0], sibling)
    copy.start()
    near.append(copy)
    for k in range(1, chips):
        source = lax.rem(chip + chips - k, chips) * 2 + core
        far[k - 1].wait_recv()
        copy = remote(out.at[source], out.at[source], near_send.at[k], near_recv.at[k], sibling)
        copy.start()
        near.append(copy)
    for copy in near:
        copy.wait_recv()
    for copy in far + near:
        copy.wait_send()


def scatter_sum(part, paired, stage, land, send, recv, near_send, near_recv, nv):
    v, w = place()
    chips = nv // 2
    chip, core = v // 2, lax.rem(v, 2)
    sibling = (chip * 2 + 1 - core, w)
    near, far = [None] * chips, []
    order = list(range(1, chips)) + [0]
    for k in order:
        to_chip = lax.rem(chip + k, chips)
        copy = remote(
            part.at[to_chip, 1 - core], paired.at[k], near_send.at[k], near_recv.at[k], sibling
        )
        copy.start()
        near[k] = copy
    total = None
    for k in order:
        to_chip = lax.rem(chip + k, chips)
        near[k].wait_recv()
        both = part[to_chip, core].astype(F32) + paired[k].astype(F32)
        if k == 0:
            total = both
        else:
            stage[k] = both.astype(BF16)
            copy = remote(stage.at[k], land.at[k], send.at[k], recv.at[k], (to_chip * 2 + core, w))
            copy.start()
            far.append(copy)
    for k in range(1, chips):
        far[k - 1].wait_recv()
        total = total + land[k].astype(F32)
    for copy in near + far:
        copy.wait_send()
    return total


def pre_kernel(nv, nw, model, hidden, gains, normed, scale, slots, ss, sr, gs, gr, hs, hr):
    v, _ = place()
    greet(column_peers(nv) + row_peers(nw))
    inputs = hidden[...].astype(F32)
    squares = row_sum(jnp.sum(inputs * inputs, axis=1, keepdims=True), slots, ss, sr, nw)
    factor = lax.rsqrt(squares / model + EPS)
    scale[...] = jnp.broadcast_to(factor, scale.shape)
    normed[v] = (inputs * factor * gains[0:1]).astype(BF16)
    gather_rows(normed, gs, gr, hs, hr, nv)


def gate_kernel(nw, gate_part, up_part, active, value, slope, mine, land, send, recv):
    v, w = place()
    greet(row_peers(nw))
    copies = []
    for half, part in enumerate((gate_part, up_part)):
        mine[half] = part[...].astype(BF16)
        for k in range(1, nw):
            copy = remote(
                mine.at[half],
                land.at[k - 1, half],
                send.at[k, half],
                recv.at[k, half],
                (v, lax.rem(w + k, nw)),
            )
            copy.start()
            copies.append(copy)
    gate, upward = gate_part[...], up_part[...]
    for copy in copies:
        copy.wait()
    for k in range(nw - 1):
        gate = gate + land[k, 0].astype(F32)
        upward = upward + land[k, 1].astype(F32)
    bent = jnp.tanh(ROOT_TWO_PI * (gate + 0.044715 * gate * gate * gate))
    gelu = 0.5 * gate * (1.0 + bent)
    active[...] = (gelu * upward).astype(BF16)
    value[...] = gelu
    slope[...] = upward * (
        0.5 * (1.0 + bent)
        + 0.5 * gate * (1.0 - bent * bent) * ROOT_TWO_PI * (1.0 + 3.0 * 0.044715 * gate * gate)
    )


def post_kernel(
    nv, nw, model,
    part, hidden, gains,
    final, branch_out, resid_out, scales,
    paired, stage, land, slots, slots_two,
    ss, sr, ts, tr, gs, gr, hs, hr, ps, pr, qs, qr,
):
    v, _ = place()
    greet(column_peers(nv) + row_peers(nw))
    branch = scatter_sum(part, paired, stage, land, ps, pr, qs, qr, nv)
    squares = row_sum(jnp.sum(branch * branch, axis=1, keepdims=True), slots, ss, sr, nw)
    scale_post = lax.rsqrt(squares / model + EPS)
    resid = hidden[...].astype(F32) + branch * scale_post * gains[1:2]
    squares = row_sum(jnp.sum(resid * resid, axis=1, keepdims=True), slots_two, ts, tr, nw)
    scale_final = lax.rsqrt(squares / model + EPS)
    final[v] = (resid * scale_final * gains[2:3]).astype(BF16)
    branch_out[...] = branch
    resid_out[...] = resid
    scales[0] = jnp.broadcast_to(scale_post, scales.shape[1:])
    scales[1] = jnp.broadcast_to(scale_final, scales.shape[1:])
    gather_rows(final, gs, gr, hs, hr, nv)


def head_kernel(
    nv, nw,
    final, head, ids, weights,
    delta, loss, part,
    held, mine, land, col_slots, row_slots, capped, total,
    ls, xs, xr, cs, cr, rs, rr, ds, dr,
):
    v, w = place()
    chunks, tokens, width = capped.shape
    sub = chunks * width

    def columns(peer, j):
        return pl.ds(pl.multiple_of(peer * sub + j * width, 128), width)

    loads = {}
    for k in list(range(1, nw)) + [0]:
        for j in range(chunks):
            where = columns(lax.rem(w + k, nw), j)
            loads[k, j] = pltpu.make_async_copy(head.at[:, where], held.at[:, where], ls.at[k, j])
            loads[k, j].start()
    column = [(lax.rem(v + k, nv), w) for k in range(1, nv)]
    row = row_peers(nw)
    greet(column + row)
    sent = {}
    for k in range(1, nw):
        peer = lax.rem(w + k, nw)
        for j in range(chunks):
            loads[k, j].wait()
            mine[k - 1, j] = jnp.dot(
                final[...], held[:, columns(peer, j)], preferred_element_type=F32
            ).astype(BF16)
            sent[k, j] = remote(
                mine.at[k - 1, j], land.at[k - 1, j], xs.at[k, j], xr.at[k, j], (v, peer)
            )
            sent[k, j].start()
    for j in range(chunks):
        loads[0, j].wait()
        capped[j] = jnp.dot(final[...], held[:, columns(w, j)], preferred_element_type=F32)
    first = (v * nw + w) * sub
    lanes = lax.broadcasted_iota(jnp.int32, (tokens, width), 1)
    sums = jnp.zeros((tokens, 1), F32)
    marks = jnp.zeros((tokens, 1), F32)
    for j in range(chunks):
        logits = capped[j]
        for k in range(1, nw):
            sent[k, j].wait()
            logits = logits + land[k - 1, j].astype(F32)
        cap = CAP * jnp.tanh(logits / CAP)
        capped[j] = cap
        hits = lanes + (first + j * width) == ids[...]
        sums = sums + jnp.sum(jnp.exp(cap - CAP), axis=1, keepdims=True)
        marks = marks + jnp.sum(jnp.where(hits, cap, 0.0), axis=1, keepdims=True)
    which = lax.broadcasted_iota(jnp.int32, (tokens, 128), 1)
    both = jnp.where(which == 0, sums, jnp.where(which == 1, marks, 0.0))
    col_slots[v] = jnp.transpose(both)[:8]
    copies = []
    for k in range(1, nv):
        copy = remote(col_slots.at[v], col_slots.at[v], cs.at[k], cr.at[k], column[k - 1])
        copy.start()
        copies.append(copy)
    for copy in copies:
        copy.wait()
    row_slots[w] = jnp.sum(col_slots[...], axis=0)
    copies = []
    for k in range(1, nw):
        copy = remote(row_slots.at[w], row_slots.at[w], rs.at[k], rr.at[k], row[k - 1])
        copy.start()
        copies.append(copy)
    for copy in copies:
        copy.wait()
    both = jnp.sum(row_slots[...], axis=0)
    both = jnp.transpose(jnp.concatenate([both] * 16, axis=0))
    lognorm = CAP + jnp.log(both[:, 0:1])
    weight = weights[...]
    logprob = both[:, 1:2] - lognorm
    mean = -jnp.sum(weight * logprob, axis=0, keepdims=True) / tokens
    loss[...] = jnp.broadcast_to(mean, loss.shape)
    sent = {}
    for j in range(chunks):
        cap = capped[j]
        hits = lanes + (first + j * width) == ids[...]
        prob = jnp.exp(cap - lognorm)
        slope = 1.0 - (cap / CAP) ** 2
        where = columns(w, j)
        delta[:, where] = (-weight * (jnp.where(hits, 1.0, 0.0) - prob) * slope).astype(BF16)
        for k in range(1, nw):
            sent[k, j] = remote(
                delta.at[:, where], delta.at[:, where], ds.at[k, j], dr.at[k, j], row[k - 1]
            )
            sent[k, j].start()
    for k in range(nw):
        source = lax.rem(w + nw - k, nw)
        for j in range(chunks):
            where = columns(source, j)
            if k:
                remote(
                    delta.at[:, where], delta.at[:, where], ds.at[k, j], dr.at[k, j], row[k - 1]
                ).wait_recv()
            rows = contract(delta[:, where], held[:, where], 1, 1)
            if k == 0 and j == 0:
                total[...] = rows
            elif k == nw - 1 and j == chunks - 1:
                part[...] = (total[...] + rows).astype(BF16)
            else:
                total[...] += rows
    for copy in sent.values():
        copy.wait_send()


def turn_kernel(
    nv, nw, model,
    part, branch_ref, resid_ref, scales, gains,
    grad_branch, grad_resid_out,
    paired, stage, land, slots, slots_two,
    ss, sr, ts, tr, gs, gr, hs, hr, ps, pr, qs, qr,
):
    v, _ = place()
    greet(column_peers(nv) + row_peers(nw))
    grad_final = scatter_sum(part, paired, stage, land, ps, pr, qs, qr, nv)
    resid, branch = resid_ref[...], branch_ref[...]
    scale_post, scale_final = scales[0][:, :1], scales[1][:, :1]
    weighted = grad_final * gains[2:3]
    back = row_sum(jnp.sum(weighted * resid, axis=1, keepdims=True), slots, ss, sr, nw)
    grad_resid = scale_final * weighted - resid * (
        scale_final * scale_final * scale_final * back / model
    )
    weighted = grad_resid * gains[1:2]
    back = row_sum(jnp.sum(weighted * branch, axis=1, keepdims=True), slots_two, ts, tr, nw)
    grad_branch[v] = (
        scale_post * weighted - branch * (scale_post * scale_post * scale_post * back / model)
    ).astype(BF16)
    grad_resid_out[...] = grad_resid
    gather_rows(grad_branch, gs, gr, hs, hr, nv)


def active_kernel(nw, part, value, slope, gate_in, up_in, mine, land, send, recv):
    v, w = place()
    greet(row_peers(nw))
    mine[...] = part[...].astype(BF16)
    copies = []
    for k in range(1, nw):
        copy = remote(mine, land.at[k - 1], send.at[k], recv.at[k], (v, lax.rem(w + k, nw)))
        copy.start()
        copies.append(copy)
    for copy in copies:
        copy.wait()
    total = part[...]
    for k in range(nw - 1):
        total = total + land[k].astype(F32)
    gate_in[...] = (total * slope[...]).astype(BF16)
    up_in[...] = (total * value[...]).astype(BF16)


def tail_kernel(
    nv, nw, model,
    part, hidden, gains, scale, grad_resid,
    out,
    paired, stage, land, slots,
    ss, sr, ps, pr, qs, qr,
):
    greet(column_peers(nv) + row_peers(nw))
    grad_normed = scatter_sum(part, paired, stage, land, ps, pr, qs, qr, nv)
    inputs = hidden[...].astype(F32)
    factor = scale[...][:, :1]
    weighted = grad_normed * gains[0:1]
    back = row_sum(jnp.sum(weighted * inputs, axis=1, keepdims=True), slots, ss, sr, nw)
    out[...] = (
        grad_resid[...]
        + factor * weighted
        - inputs * (factor * factor * factor * back / model)
    ).astype(BF16)


def call(kernel, number, outs, scratch, name, whole=()):
    vmem = pl.BlockSpec(memory_space=pltpu.VMEM)

    def run(*operands):
        return pl.pallas_call(
            kernel,
            out_shape=tuple(jax.ShapeDtypeStruct(shape, kind) for shape, kind in outs),
            in_specs=[
                pl.BlockSpec(memory_space=pl.ANY) if i in whole else vmem
                for i in range(len(operands))
            ],
            out_specs=tuple(vmem for _ in outs),
            scratch_shapes=scratch,
            compiler_params=pltpu.CompilerParams(
                collective_id=number, has_side_effects=True, vmem_limit_bytes=LIMIT
            ),
            name=name,
        )(*operands)

    return run


def shards(
    hidden,
    pre_gain,
    post_gain,
    final_gain,
    gate_weight,
    up_weight,
    down_weight,
    head_weight,
    token_ids,
    rewards,
):
    nv, nw = lax.axis_size("vocab"), lax.axis_size("width")
    own, wide = hidden.shape
    model = wide * nw
    tokens = nv * own
    chips = nv // 2
    units = gate_weight.shape[1]
    vocab_dev = head_weight.shape[1]
    sub = vocab_dev // nw
    gains = jnp.stack([pre_gain, post_gain, final_gain])

    sums = pltpu.VMEM((nw, own, 128), F32)
    row_sems = [DMA((nw,)), DMA((nw,))]
    chip_sems = [DMA((chips,)), DMA((chips,))]
    block = pltpu.VMEM((chips, own, wide), BF16)
    gather_sems = chip_sems * 2

    normed, scale = call(
        functools.partial(pre_kernel, nv, nw, model),
        0,
        [((nv, own, wide), BF16), ((own, 128), F32)],
        [sums] + row_sems + gather_sems,
        "pre_norm",
    )(hidden, gains)
    normed = normed.reshape(tokens, wide)
    gate_part = jnp.dot(normed, gate_weight, preferred_element_type=F32)
    up_part = jnp.dot(normed, up_weight, preferred_element_type=F32)
    active, value, slope = call(
        functools.partial(gate_kernel, nw),
        1,
        [((tokens, units), BF16), ((tokens, units), F32), ((tokens, units), F32)],
        [
            pltpu.VMEM((2, tokens, units), BF16),
            pltpu.VMEM((nw - 1, 2, tokens, units), BF16),
            DMA((nw, 2)),
            DMA((nw, 2)),
        ],
        "gate_sum",
    )(gate_part, up_part)
    branch_part = jnp.dot(active, down_weight, preferred_element_type=F32).astype(BF16)
    final, branch, resid, scales = call(
        functools.partial(post_kernel, nv, nw, model),
        2,
        [((nv, own, wide), BF16), ((own, wide), F32), ((own, wide), F32), ((2, own, 128), F32)],
        [block, block, block, sums, sums] + row_sems * 2 + gather_sems + chip_sems * 2,
        "post_norm",
    )(branch_part.reshape(chips, 2, own, wide), hidden, gains)
    final = final.reshape(tokens, wide)
    weights = jnp.repeat(rewards, tokens // rewards.shape[0])[:, None]
    width = min(512, sub)
    chunks = sub // width
    sems = [DMA((nw, chunks)), DMA((nw, chunks))]
    delta, loss, final_part = call(
        functools.partial(head_kernel, nv, nw),
        3,
        [((tokens, vocab_dev), BF16), ((8, 128), F32), ((tokens, wide), BF16)],
        [
            pltpu.VMEM((wide, vocab_dev), BF16),
            pltpu.VMEM((nw - 1, chunks, tokens, width), BF16),
            pltpu.VMEM((nw - 1, chunks, tokens, width), BF16),
            pltpu.VMEM((nv, 8, tokens), F32),
            pltpu.VMEM((nw, 8, tokens), F32),
            pltpu.VMEM((chunks, tokens, width), F32),
            pltpu.VMEM((tokens, wide), F32),
            DMA((nw, chunks)),
        ]
        + sems
        + [DMA((nv,)), DMA((nv,))]
        + row_sems
        + sems,
        "head_loss",
        whole=(1,),
    )(final, head_weight, token_ids[:, None], weights)
    grad_branch, grad_resid = call(
        functools.partial(turn_kernel, nv, nw, model),
        4,
        [((nv, own, wide), BF16), ((own, wide), F32)],
        [block, block, block, sums, sums] + row_sems * 2 + gather_sems + chip_sems * 2,
        "turn",
    )(final_part.reshape(chips, 2, own, wide), branch, resid, scales, gains)
    grad_branch = grad_branch.reshape(tokens, wide)
    active_part = contract(grad_branch, down_weight, 1, 1)
    gate_in, up_in = call(
        functools.partial(active_kernel, nw),
        5,
        [((tokens, units), BF16), ((tokens, units), BF16)],
        [
            pltpu.VMEM((tokens, units), BF16),
            pltpu.VMEM((nw - 1, tokens, units), BF16),
        ]
        + row_sems,
        "active_sum",
    )(active_part, value, slope)
    normed_part = (
        contract(gate_in, gate_weight, 1, 1) + contract(up_in, up_weight, 1, 1)
    ).astype(BF16)
    (grad_hidden,) = call(
        functools.partial(tail_kernel, nv, nw, model),
        6,
        [((own, wide), BF16)],
        [block, block, block, sums] + row_sems + chip_sems * 2,
        "tail",
    )(normed_part.reshape(chips, 2, own, wide), hidden, gains, scale, grad_resid)
    grad_head = contract(final, delta, 0, 0).astype(BF16)
    grad_down = contract(active, grad_branch, 0, 0).astype(BF16)
    grad_gate = contract(normed, gate_in, 0, 0).astype(BF16)
    grad_up = contract(normed, up_in, 0, 0).astype(BF16)
    return (grad_hidden, grad_gate, grad_up, grad_down, grad_head, loss[0, 0])


def solution(mesh):
    return jax.shard_map(
        shards,
        mesh=mesh,
        in_specs=(
            P("vocab", "width"),
            P("width"),
            P("width"),
            P("width"),
            P("width", "vocab"),
            P("width", "vocab"),
            P("vocab", "width"),
            P("width", "vocab"),
            P(),
            P(),
        ),
        out_specs=(
            P("vocab", "width"),
            P("width", "vocab"),
            P("width", "vocab"),
            P("vocab", "width"),
            P("width", "vocab"),
            P(),
        ),
        check_vma=False,
    )
```
